256 devices in a mesh: gx: 8 (over z_lo, y), gy: 4 (over x), gz: 8 (over z_hi, core).
Axes of the slice: x: 4, y: 4, z: 8 (z_hi: 4, z_lo: 2; z = z_hi * 2 + z_lo), core: 2. Of those that a mesh axis runs over, the one named last changes fastest.
Arguments:
- layer_input: bfloat16 [6144, 8192], P(('gz', 'gy'), 'gx'), may hold values from -0.15625 to 0.15625
- core_output: bfloat16 [6144, 8192], P(('gz', 'gy'), 'gx'), may hold values from -0.15625 to 0.15625
- grad_qkv: bfloat16 [6144, 9216], P(('gz', 'gx'), 'gy'), may hold values from -6 to 6
- grad_out: bfloat16 [6144, 8192], P(('gz', 'gx'), 'gy'), may hold values from -6 to 6
- w_qkv: bfloat16 [8192, 9216], P(('gx', 'gz'), 'gy'), may hold values from -0.0625 to 0.0625
- w_out: bfloat16 [8192, 8192], P(('gx', 'gz'), 'gy'), may hold values from -0.0625 to 0.0625
Outputs:
- grad_input: bfloat16 [6144, 8192], P(('gz', 'gy'), 'gx')
- grad_core: bfloat16 [6144, 8192], P(('gz', 'gy'), 'gx')
- grad_w_qkv: bfloat16 [8192, 9216], P(('gx', 'gz'), 'gy')
- grad_w_out: bfloat16 [8192, 8192], P(('gx', 'gz'), 'gy')
The draws below stay inside these ranges and needn't reach their ends.
All inputs are finite; a program needn't handle non-finite values.
Results may differ from the reference program's by a relative error of at most 0.017.
Values may be sent and summed in bfloat16 or wider, within the bound.
No kernel may reach another device: no remote copies, remote signals or barrier semaphores. Data moves between devices by JAX's collectives and lax.ppermute only.
A program may use at most 192 MiB of HBM per device.

```python
import jax
import jax.numpy as jnp
from jax import lax

D = 8192
TOK_BLK = 768
HQ = 8192
NQKV = 9216
TOKENS = 6144
N_GY = 4
N_GZ = 8


def strengthened(drawn, rng, source, target, parts, factor):
    owner, partner = [(jnp.arange(drawn.shape[dim]) // (drawn.shape[dim] // parts)).reshape([-1 if axis == dim else 1 for axis in range(drawn.ndim)]) for dim in (source, target)]
    chosen = jax.random.permutation(rng, parts)[partner]
    strong = (owner == chosen) | (owner == (partner + parts // 2) % parts)
    return jnp.where(strong, factor * drawn, drawn)


def shard_levels(own_key, shape, shards, smallest, largest):
    gain, own = 1.0, jax.random.fold_in(own_key, 6)
    for position, blocks in shards:
        steps = jnp.exp(jax.random.uniform(jax.random.fold_in(own, position), (blocks,), jnp.float32, smallest / len(shards), largest / len(shards)))
        gain = gain * jnp.repeat(steps, shape[position] // blocks).reshape([-1 if axis == position else 1 for axis in range(len(shape))])
    return gain


def centred(key, shape, deviation, reach, shards=(), dtype=jnp.bfloat16):
    gain = shard_levels(key, shape, shards, -0.22, 0.18) if shards else 1.0
    entries = jax.random.normal(key, shape, jnp.float32) * deviation * gain
    return jnp.minimum(jnp.maximum(entries, -reach), reach).astype(dtype)


def noise_with(own_key, shape, deviation, most, split, heavy, dtype=jnp.bfloat16):
    result = deviation * jax.random.normal(own_key, shape, jnp.float32)
    if split:
        result = result * shard_levels(own_key, shape, split, -0.22, 0.18)
    return jnp.clip(strengthened(result, jax.random.fold_in(own_key, 3), *heavy), -most, most).astype(dtype)


def setup_inputs(seed: int = 0) -> dict:
    splits = jax.random.split(jax.random.key(seed), 7)
    return {
        "layer_input": noise_with(splits[0], (TOKENS, D), TOKENS ** -0.5, 0.15625, ((0, 32), (1, 8)), (0, 1, 32, 2.75)),
        "core_output": noise_with(splits[1], (TOKENS, HQ), TOKENS ** -0.5, 0.15625, ((0, 32), (1, 8)), (0, 1, 32, 2.75)),
        "grad_qkv": centred(splits[2], (TOKENS, NQKV), 1.0, 6.0, ((0, 64), (1, 4))),
        "grad_out": centred(splits[3], (TOKENS, D), 1.0, 6.0, ((0, 64), (1, 4))),
        "w_qkv": centred(splits[4], (D, NQKV), D ** -0.5, 0.0625, ((0, 64), (1, 4))),
        "w_out": centred(splits[5], (HQ, D), HQ ** -0.5, 0.0625, ((0, 64), (1, 4))),
    }


def backward_pair(inp, gout, weight):
    width = gout.shape[1] // N_GY
    d_inp = jnp.zeros((inp.shape[0], inp.shape[1]), jnp.float32)
    for j in range(N_GY):
        cols = gout[:, j * width:(j + 1) * width]
        wcols = weight[:, j * width:(j + 1) * width]
        part = lax.optimization_barrier(jnp.einsum("tn,kn->tk", cols, wcols, preferred_element_type=jnp.float32).astype(jnp.bfloat16))
        d_inp = d_inp + part.astype(jnp.float32)
    d_w = jnp.zeros((weight.shape[0], weight.shape[1]), jnp.float32)
    for b in range(N_GZ):
        rows_in = inp[b * TOK_BLK:(b + 1) * TOK_BLK]
        rows_g = gout[b * TOK_BLK:(b + 1) * TOK_BLK]
        part = lax.optimization_barrier(jnp.einsum("tk,tn->kn", rows_in, rows_g, preferred_element_type=jnp.float32).astype(jnp.bfloat16))
        d_w = d_w + part.astype(jnp.float32)
    return d_inp.astype(jnp.bfloat16), d_w.astype(jnp.bfloat16)


def reference(layer_input, core_output, grad_qkv, grad_out, w_qkv, w_out):
    grad_input, grad_w_qkv = backward_pair(layer_input, grad_qkv, w_qkv)
    grad_core, grad_w_out = backward_pair(core_output, grad_out, w_out)
    return (grad_input, grad_core, grad_w_qkv, grad_w_out)
```

```python
import jax
import jax.numpy as jnp
from jax import lax
from jax.sharding import Mesh, PartitionSpec as P

AXES = ("zl", "y", "x", "zh", "c")
SIZES = (2, 4, 4, 4, 2)


def place(i):
    c = i % 2
    zh = (i // 2) % 4
    x = (i // 8) % 4
    y = (i // 32) % 4
    zl = i // 128
    return zl, y, x, zh, c


def number(zl, y, x, zh, c):
    return (((zl * 4 + y) * 4 + x) * 4 + zh) * 2 + c


def permute(value, target):
    pairs = [(i, number(*target(*place(i)))) for i in range(256)]
    return lax.ppermute(value, AXES, pairs)


def ring_x(zl, y, x, zh, c):
    return zl, y, (x + 1 - 2 * c) % 4, zh, c


def ring_y(zl, y, x, zh, c):
    return zl, (y + 1 - 2 * c) % 4, x, zh, c


def ring_z(zl, y, x, zh, c):
    z = (zh * 2 + zl + 1 - 2 * c) % 8
    return z % 2, y, x, z // 2, c


def other_core(zl, y, x, zh, c):
    return zl, y, x, zh, 1 - c


def shift_zh(r):
    return lambda zl, y, x, zh, c: (zl, y, x, zh ^ r, c)


def spread_xy(r):
    def target(zl, y, x, zh, c):
        q = y ^ r
        return zl, (x % 2) * 2 + q % 2, (x // 2) * 2 + q // 2, zh, c

    return target


def collect_xy(r):
    def target(zl, y, x, zh, c):
        q = ((x % 2) * 2 + y % 2) ^ r
        return zl, q, (x // 2) * 2 + y // 2, zh, c

    return target


def put(buffer, block, index):
    return lax.dynamic_update_index_in_dim(buffer, block, index, 0)


def take(buffer, index, axis=0):
    return lax.dynamic_index_in_dim(buffer, index, axis, keepdims=False)


def add(a, b):
    return (a.astype(jnp.float32) + b.astype(jnp.float32)).astype(jnp.bfloat16)


def body(layer_input, core_output, grad_qkv, grad_out, w_qkv, w_out):
    zl, y, x, zh, c = (lax.axis_index(a) for a in AXES)
    z = zh * 2 + zl
    way = 1 - 2 * c
    piece = grad_qkv.shape[0]
    lanes = w_qkv.shape[0]

    gs, ws = [], []
    for g in (grad_qkv, grad_out):
        held = g
        full = put(jnp.zeros((8,) + g.shape, g.dtype), held, z)
        for step in range(1, 8):
            held = permute(held, ring_z)
            full = put(full, held, (z - way * step) % 8)
        gs.append(full)
    for w in (w_qkv, w_out):
        held = w
        own = put(jnp.zeros((4,) + w.shape, w.dtype), held, y)
        for step in range(1, 4):
            held = permute(held, ring_y)
            own = put(own, held, (y - way * step) % 4)
        other = permute(own, other_core)
        first = jnp.where(c == 0, own, other)
        second = jnp.where(c == 0, other, own)
        ws.append(jnp.stack([first, second], axis=1).reshape(8 * lanes, w.shape[1]))

    xs = jnp.stack([layer_input, core_output])
    xs = xs.reshape(2, 2, piece, 4, 2 * lanes)
    got = jnp.zeros((4, 2, 2, piece, 2 * lanes), xs.dtype)
    for r in range(4):
        sent = take(xs, zh ^ r, 3)
        got = put(got, permute(sent, shift_zh(r)) if r else sent, zh ^ r)
    got = got.reshape(2, 2, 2, 2, piece, 2 * lanes)
    spread = jnp.zeros((4, 2, 2, piece, 2 * lanes), xs.dtype)
    for r in range(4):
        q = y ^ r
        sent = take(take(got, q // 2, 0), q % 2, 2)
        mine = (x % 2) * 2 + y % 2
        spread = put(spread, permute(sent, spread_xy(r)), mine ^ r)
    inputs = []
    for a in range(2):
        held = spread[:, :, a].transpose(1, 2, 0, 3).reshape(2, piece, 8 * lanes)
        full = put(jnp.zeros((4,) + held.shape, held.dtype), held, x)
        for step in range(1, 4):
            held = permute(held, ring_x)
            full = put(full, held, (x - way * step) % 4)
        full = full.reshape(2, 2, 2, piece, 8 * lanes).transpose(1, 2, 0, 3, 4)
        inputs.append(full.reshape(8 * piece, 8 * lanes))

    d_inputs, d_weights = [], []
    for inp, g, w in zip(inputs, gs, ws):
        n = w.shape[1]
        rows = g.reshape(8 * piece, n)
        part = jnp.einsum("tn,kn->tk", rows, w, preferred_element_type=jnp.float32).astype(jnp.bfloat16)
        part = part.reshape(2, 2, 2, piece, 8 * lanes).transpose(2, 0, 1, 3, 4).reshape(4, 2, piece, 8 * lanes)
        total = take(part, (x - way) % 4)
        for step in range(2, 5):
            total = add(permute(total, ring_x), take(part, (x - way * step) % 4))
        total = total.reshape(2, piece, 4, 2 * lanes)
        back = jnp.zeros((4, 2, piece, 2 * lanes), total.dtype)
        for r in range(4):
            sent = take(total, ((x % 2) * 2 + y % 2) ^ r, 2)
            back = put(back, permute(sent, collect_xy(r)), y ^ r)
        back = back.reshape(2, 2, 2, piece, 2 * lanes).transpose(0, 2, 1, 3, 4)
        back = back.reshape(4, 2 * piece, 2 * lanes)
        out = jnp.zeros((4, 2 * piece, 2 * lanes), total.dtype)
        for r in range(4):
            sent = take(back, zh ^ r)
            out = put(out, permute(sent, shift_zh(r)) if r else sent, zh ^ r)
        d_inputs.append(out.transpose(1, 0, 2).reshape(2 * piece, 8 * lanes))

        part = jnp.einsum("tk,tn->kn", inp, rows, preferred_element_type=jnp.float32).astype(jnp.bfloat16)
        part = part.reshape(4, 2, lanes, n)
        part = add(take(part, c, 1), permute(take(part, 1 - c, 1), other_core))
        total = take(part, (y - way) % 4)
        for step in range(2, 5):
            total = add(permute(total, ring_y), take(part, (y - way * step) % 4))
        d_weights.append(total)
    return d_inputs[0], d_inputs[1], d_weights[0], d_weights[1]


def solution(mesh):
    fine = Mesh(mesh.devices.reshape(SIZES), AXES)
    inputs = P(("zh", "c", "x"), ("zl", "y"))
    grads = P(("zh", "c", "zl", "y"), "x")
    weights = P(("zl", "y", "zh", "c"), "x")
    return jax.shard_map(
        body,
        mesh=fine,
        in_specs=(inputs, inputs, grads, grads, weights, weights),
        out_specs=(inputs, inputs, weights, weights),
        check_vma=False,
    )
```

```python
import jax
import jax.numpy as jnp
from jax import lax
from jax.experimental import pallas as pl
from jax.experimental.pallas import tpu as pltpu
from jax.sharding import Mesh, PartitionSpec as P

AXES = ("zl", "y", "x", "zh", "c")
SIZES = (2, 4, 4, 4, 2)


def place(i):
    return (i // 128) % 2, (i // 32) % 4, (i // 8) % 4, (i // 2) % 4, i % 2


def number(zl, y, x, zh, c):
    return (((zl * 4 + y) * 4 + x) * 4 + zh) * 2 + c


def permute(value, target):
    pairs = [(i, number(*target(*place(i)))) for i in range(256)]
    return lax.ppermute(value, AXES, pairs)


def pair_x(r):
    return lambda zl, y, x, zh, c: (zl, y, x ^ r, zh, c)


def pair_y(r):
    return lambda zl, y, x, zh, c: (zl, y ^ r, x, zh, c)


def other_core(zl, y, x, zh, c):
    return zl, y, x, zh, 1 - c


def shift_y(step):
    return lambda zl, y, x, zh, c: (zl, (y + step) % 4, x, zh, c)


def ring_z(zl, y, x, zh, c):
    z = (zh * 2 + zl + 1 - 2 * c) % 8
    return z % 2, y, x, z // 2, c


def spread_xy(r):
    def target(zl, y, x, zh, c):
        xh, xl, yh, yl = x // 2, x % 2, y // 2, y % 2
        return zl, xl * 2 + (yl ^ r), xh * 2 + (yh ^ xh), zh, c

    return target


def collect_xy(r):
    def target(zl, y, x, zh, c):
        xh, xl, yh, yl = x // 2, x % 2, y // 2, y % 2
        return zl, (xl ^ xh) * 2 + (yl ^ r), xh * 2 + yh, zh, c

    return target


def swap_blocks(value):
    return lax.all_to_all(value, "zh", 0, 0, tiled=True)


def either(bit, first, second):
    return jnp.where(bit == 0, first, second)


def add(a, b):
    return (a.astype(jnp.float32) + b.astype(jnp.float32)).astype(jnp.bfloat16)


def tie(*values):
    return lax.optimization_barrier(values)


def dot(a, b, on):
    return lax.dot_general(a, b, (on, ((), ())), preferred_element_type=jnp.float32).astype(jnp.bfloat16)


def call(kernel, operands, out_shape, scratch, copies, flops):
    moved = sum(v.size * 2 for v in operands) + out_shape.size * 2
    return pl.pallas_call(
        kernel,
        out_shape=out_shape,
        in_specs=[pl.BlockSpec(memory_space=pl.ANY)] * len(operands),
        out_specs=pl.BlockSpec(memory_space=pltpu.VMEM),
        scratch_shapes=scratch + [pltpu.SemaphoreType.DMA((copies,))],
        compiler_params=pltpu.CompilerParams(vmem_limit_bytes=40 * 1024 * 1024),
        cost_estimate=pl.CostEstimate(flops=flops, bytes_accessed=moved, transcendentals=0),
    )(*operands)


def load_rows(refs, target, sems, first_sem, spots):
    copies = []
    for i, (ref, spot) in enumerate(zip(refs, spots)):
        copy = pltpu.make_async_copy(ref, target.at[spot], sems.at[first_sem + i])
        copy.start()
        copies.append(copy)
    return copies


def back_to_inputs(rows, weights, starts, spots_of, n, lanes, halves):
    piece = rows[0].shape[0]
    used_rows = sorted({t for t, _ in halves})
    used_cols = sorted({f for _, f in halves})

    def kernel(*refs):
        row_refs, weight_refs, out = refs[:8], refs[8:16], refs[16]
        held_rows, held_weights, sems = refs[17:]
        row_spots, weight_spots = spots_of()
        weight_copies = []
        for i, (ref, spot) in enumerate(zip(weight_refs, weight_spots)):
            source = ref.at[:, pl.ds(starts[i], n)]
            copy = pltpu.make_async_copy(source, held_weights.at[spot], sems.at[8 + i])
            copy.start()
            weight_copies.append(copy)
        row_copies = load_rows(row_refs, held_rows, sems, 0, row_spots)
        for copy in weight_copies + row_copies:
            copy.wait()
        for i, (t, f) in enumerate(halves):
            a = held_rows[4 * t : 4 * t + 4].reshape(4 * piece, n)
            b = held_weights[4 * f : 4 * f + 4].reshape(4 * lanes, n)
            out[i] = dot(a, b, ((1,), (1,)))

    scratch = [pltpu.VMEM((8, piece, n), jnp.bfloat16), pltpu.VMEM((8, lanes, n), jnp.bfloat16)]
    out_shape = jax.ShapeDtypeStruct((2, 4 * piece, 4 * lanes), jnp.bfloat16)
    flops = 2 * 2 * 4 * piece * 4 * lanes * n
    return call(kernel, list(rows) + list(weights), out_shape, scratch, 16, flops)


def back_to_weights(rows, pieces, spots_of, n, lanes, block):
    piece = rows[0].shape[0]
    width = block

    def kernel(*refs):
        row_refs, piece_refs, out = refs[:8], refs[8:12], refs[12]
        held_rows, held_pieces, turned, sems = refs[13:]
        row_spots, piece_spots, core = spots_of()
        copies = []
        for i, (ref, spots) in enumerate(zip(piece_refs, piece_spots)):
            token, order = spots
            for r in range(2):
                source = ref.at[r, :, pl.ds(pl.multiple_of(core * lanes, lanes), lanes)]
                target = held_pieces.at[order[r], pl.ds(pl.multiple_of(token * 4 * piece, 4 * piece), 4 * piece), :]
                copy = pltpu.make_async_copy(source, target, sems.at[8 + 2 * i + r])
                copy.start()
                copies.append(copy)
        row_copies = load_rows(row_refs, held_rows, sems, 0, row_spots)
        for copy in copies:
            copy.wait()
        for i in range(4):
            turned[i * lanes : (i + 1) * lanes, :] = held_pieces[i].T
        for copy in row_copies:
            copy.wait()
        for i in range(n // width):
            cols = held_rows[:, :, i * width : (i + 1) * width].reshape(8 * piece, width)
            out[:, i * width : (i + 1) * width] = dot(turned[...], cols, ((1,), (0,)))

    scratch = [
        pltpu.VMEM((8, piece, n), jnp.bfloat16),
        pltpu.VMEM((4, 8 * piece, lanes), jnp.bfloat16),
        pltpu.VMEM((4 * lanes, 8 * piece), jnp.bfloat16),
    ]
    out_shape = jax.ShapeDtypeStruct((4 * lanes, n), jnp.bfloat16)
    flops = 2 * 4 * lanes * 8 * piece * n
    return call(kernel, list(rows) + list(pieces), out_shape, scratch, 16, flops)


def body(layer_input, core_output, grad_qkv, grad_out, w_qkv, w_out):
    def me():
        zl, y, x, zh, c = (lax.axis_index(a) for a in AXES)
        return zl, y, x, zh, c, lax.rem(lax.div(y, 2) + lax.rem(y, 2), 2), lax.rem(lax.div(x, 2) + lax.rem(x, 2), 2)

    yl = lax.rem(lax.axis_index("y"), 2)
    piece = grad_qkv.shape[0]
    lanes = w_qkv.shape[0]
    sizes = [w_qkv.shape[1], w_out.shape[1]]
    starts = [0, sizes[0]]

    def flip(a, b):
        return lax.rem(a + b, 2)

    def row_spots():
        zl, y, x, zh, c, p, h = me()
        z = zh * 2 + zl
        spots = []
        for step in range(8):
            at = lax.rem(z + (1 - c) * (8 - step) + c * step, 8)
            spots.append(flip(lax.rem(at, 2), lax.div(x, 2)) * 4 + lax.div(at, 2))
        return spots

    def weight_spots():
        zl, y, x, zh, c, p, h = me()
        spots = []
        for core in (c, 1 - c):
            for step in (0, 3, 1, 2):
                at = lax.rem(y + step, 4)
                spots.append(flip(lax.div(at, 2), h) * 4 + flip(lax.rem(at, 2), lax.rem(y, 2)) * 2 + core)
        return spots

    def piece_spots(places, own):
        zl, y, x, zh, c, p, h = me()
        spots = []
        for token, feature in places:
            half = flip(h, feature)
            order = []
            for r in range(2):
                low = flip(lax.rem(y, 2), r)
                rel_p = flip(flip(half, low), p)
                rel_h = flip(half, lax.div(y, 2))
                order.append(rel_p * 2 + rel_h)
            spots.append((token, order))
        return spots, (c if own else 1 - c)

    held = [grad_qkv, grad_out]
    rows = [[grad_qkv], [grad_out]]

    def hop():
        for i in range(2):
            held[i] = permute(held[i], ring_z)
            rows[i].append(held[i])

    own = jnp.concatenate([w_qkv, w_out], 1)
    hop()
    low = permute(own, shift_y(1))
    high = permute(own, shift_y(-1))
    xs = jnp.stack([layer_input, core_output]).reshape(2, 2, piece, 4, 2 * lanes)
    xs = xs.transpose(3, 1, 0, 2, 4)
    xs = swap_blocks(xs)
    held[0], xs, low, high = tie(held[0], xs, low, high)
    hop()
    across = [permute(low[:, : sizes[0]], shift_y(1)), permute(high[:, sizes[0] :], shift_y(-1))]
    far = [permute(v, other_core) for v in (own, low)]
    hop()
    held[1], xs, *across = tie(held[1], xs, *across)
    spread = [permute(either(flip(yl, r), xs[:, 0], xs[:, 1]), spread_xy(r)) for r in range(2)]
    hop()
    held[1], high, *far = tie(held[1], high, *far)
    far.append(permute(high, other_core))
    hop()
    held[1], *spread = tie(held[1], *spread)
    first = [jnp.stack([v[:, i].reshape(4 * piece, 2 * lanes) for v in spread]) for i in range(2)]
    second = [permute(first[0], pair_x(3)), permute(first[1], pair_x(1))]
    far_across = [permute(v, other_core) for v in across]
    hop()
    held[1], far[2], *far_across = tie(held[1], far[2], *far_across)
    held[1], *second = tie(held[1], *second)
    third = [jnp.stack([first[i], second[i]]) for i in range(2)]
    third = [permute(third[0], pair_x(1)), permute(third[1], pair_x(3))]
    hop()
    weights = [[own, low, high, across[i], *far, far_across[i]] for i in range(2)]
    begins = [[0, 0, 0, 0] * 2, [sizes[0], sizes[0], sizes[0], 0] * 2]

    def inputs_part(a, halves, *before):
        rows[a][0] = tie(rows[a][0], *before)[0]
        spots = lambda: (row_spots(), weight_spots())
        return back_to_inputs(rows[a], weights[a], begins[a], spots, sizes[a], lanes, halves)

    def weights_part(a, mine, *before):
        rows[a][0] = tie(rows[a][0], *before)[0]
        places = [(0, 0), (1, 0), (0, 1), (1, 1)] if a == 0 else [(0, 0), (0, 1), (1, 0), (1, 1)]
        pieces = [first[a], second[a], third[a][0], third[a][1]]

        def spots():
            chosen, core = piece_spots(places, mine)
            return row_spots(), chosen, core

        return back_to_weights(rows[a], pieces, spots, sizes[a], lanes, 256)

    one_sent = inputs_part(0, [(0, 1), (1, 1)])
    one_got = permute(one_sent, pair_x(1))
    two_sent = inputs_part(1, [(1, 0), (1, 1)], one_sent)
    two_got = permute(two_sent, pair_x(3))
    one = inputs_part(0, [(0, 0), (1, 0)], two_sent)
    two = inputs_part(1, [(0, 0), (0, 1)], one)

    def exchange(mine, got, n):
        mine, got = (v.reshape(4, lanes, n) for v in (mine, got))
        left, right = (slice(0, n // 2), slice(n // 2, n))
        pick = lambda v, blocks, cols: jnp.stack([v[b, :, cols] for b in blocks])
        sent = [add(pick(mine, (2, 3), left), pick(got, (2, 3), left)), add(pick(mine, (1, 3), right), pick(got, (1, 3), right))]
        kept = [add(pick(mine, (0, 1), left), pick(got, (0, 1), left)), add(pick(mine, (0, 2), right), pick(got, (0, 2), right))]
        return sent, kept

    def start_y(sent):
        return [permute(sent[0], pair_y(1)), permute(sent[1], pair_y(3))]

    def next_y(kept, got):
        sent = [add(k[1], g[1]) for k, g in zip(kept, got)]
        kept = [add(k[0], g[0]) for k, g in zip(kept, got)]
        return [permute(sent[0], pair_y(3)), permute(sent[1], pair_y(1))], kept

    def last_y(kept, got):
        return jnp.concatenate([add(k, g) for k, g in zip(kept, got)], -1)

    def collect(total):
        total = total.reshape(4, piece, 4 * lanes)
        return [permute(total[..., r * 2 * lanes : (r + 1) * 2 * lanes], collect_xy(r)) for r in range(2)]

    def finish(back):
        back = jnp.stack([either(yl, *back), either(yl, back[1], back[0])], 1)
        back = swap_blocks(back)
        return jnp.concatenate([back[k] for k in range(4)], -1).reshape(2 * piece, 8 * lanes)

    part_one = weights_part(0, False, two)
    got_one = permute(part_one, other_core)
    one_got, part_one = tie(one_got, part_one)
    one = add(one, one_got)
    one_got = permute(one[1], pair_x(3))
    mine_one = weights_part(0, True, one)
    two_got, mine_one = tie(two_got, mine_one)
    two = add(two, two_got)
    two_got = permute(two[1], pair_x(1))
    part_two = weights_part(1, False, two)
    got_two = permute(part_two, other_core)
    sent, kept_one = exchange(mine_one, got_one, sizes[0])
    part_two, *sent = tie(part_two, *sent)
    y_one = start_y(sent)
    one_got, sent[0] = tie(one_got, sent[0])
    one = add(one[0], one_got)
    back_one = collect(one)
    mine_two = weights_part(1, True, one)
    two_got, mine_two = tie(two_got, mine_two)
    two = add(two[0], two_got)
    back_two = collect(two)
    got_two, two = tie(got_two, two)
    sent, kept_two = exchange(mine_two, got_two, sizes[1])
    y_two = start_y(sent)
    back_one[0], sent[0] = tie(back_one[0], sent[0])
    d_one = finish(back_one)
    y_one, kept_one = next_y(kept_one, y_one)
    d_two = finish(back_two)
    y_two, kept_two = next_y(kept_two, y_two)
    return d_one, d_two, last_y(kept_one, y_one), last_y(kept_two, y_two)


def solution(mesh):
    fine = Mesh(mesh.devices.reshape(SIZES), AXES)
    inputs = P(("zh", "c", "x"), ("zl", "y"))
    grads = P(("zh", "c", "zl", "y"), "x")
    weights = P(("zl", "y", "zh", "c"), "x")
    return jax.shard_map(
        body,
        mesh=fine,
        in_specs=(inputs, inputs, grads, grads, weights, weights),
        out_specs=(inputs, inputs, weights, weights),
        check_vma=False,
    )
```

```python
import jax
import jax.numpy as jnp
from jax import lax
from jax.experimental import pallas as pl
from jax.experimental.pallas import tpu as pltpu
from jax.sharding import Mesh, PartitionSpec as P

AXES = ("zl", "y", "x", "zh", "c")
SIZES = (2, 4, 4, 4, 2)


def place(i):
    return (i // 128) % 2, (i // 32) % 4, (i // 8) % 4, (i // 2) % 4, i % 2


def number(zl, y, x, zh, c):
    return (((zl * 4 + y) * 4 + x) * 4 + zh) * 2 + c


def permute(value, target):
    pairs = [(i, number(*target(*place(i)))) for i in range(256)]
    return lax.ppermute(value, AXES, pairs)


def pair_x(r):
    return lambda zl, y, x, zh, c: (zl, y, x ^ r, zh, c)


def pair_y(r):
    return lambda zl, y, x, zh, c: (zl, y ^ r, x, zh, c)


def other_core(zl, y, x, zh, c):
    return zl, y, x, zh, 1 - c


def shift_y(step):
    return lambda zl, y, x, zh, c: (zl, (y + step) % 4, x, zh, c)


def ring_z(zl, y, x, zh, c):
    z = (zh * 2 + zl + 1 - 2 * c) % 8
    return z % 2, y, x, z // 2, c


def spread_xy(r):
    def target(zl, y, x, zh, c):
        xh, xl, yh, yl = x // 2, x % 2, y // 2, y % 2
        return zl, xl * 2 + (yl ^ r), xh * 2 + (yh ^ xh), zh, c

    return target


def collect_xy(r):
    def target(zl, y, x, zh, c):
        xh, xl, yh, yl = x // 2, x % 2, y // 2, y % 2
        return zl, (xl ^ xh) * 2 + (yl ^ r), xh * 2 + yh, zh, c

    return target


def swap_blocks(value):
    return lax.all_to_all(value, "zh", 0, 0, tiled=True)


def either(bit, first, second):
    return jnp.where(bit == 0, first, second)


def flip(a, b):
    return lax.rem(a + b, 2)


def add(a, b):
    return (a.astype(jnp.float32) + b.astype(jnp.float32)).astype(jnp.bfloat16)


def tie(*values):
    return lax.optimization_barrier(values)


def dot(a, b, on):
    return lax.dot_general(a, b, (on, ((), ())), preferred_element_type=jnp.float32)


def me():
    zl, y, x, zh, c = (lax.axis_index(a) for a in AXES)
    p = flip(lax.div(y, 2), lax.rem(y, 2))
    h = flip(lax.div(x, 2), lax.rem(x, 2))
    return zl, y, x, zh, c, p, h


def run(weight, *jobs):
    operands = [v for job in jobs for v in job[0]]
    outs = [v for job in jobs for v in job[1]]

    def kernel(*refs):
        at = [0, len(operands), len(operands) + len(outs)]
        stages = []
        for ins, out, scratch, body in jobs:
            parts = []
            for i, v in enumerate((ins, out, scratch)):
                parts.append(refs[at[i] : at[i] + len(v)])
                at[i] += len(v)
            stages.append(body(*parts))
        for finish in stages:
            finish()

    return pl.pallas_call(
        kernel,
        out_shape=outs,
        in_specs=[pl.BlockSpec(memory_space=pl.ANY)] * len(operands),
        out_specs=[pl.BlockSpec(memory_space=pltpu.VMEM)] * len(outs),
        scratch_shapes=[v for job in jobs for v in job[2]],
        compiler_params=pltpu.CompilerParams(vmem_limit_bytes=48 * 1024 * 1024),
        cost_estimate=pl.CostEstimate(flops=weight * 3_400_000_000, bytes_accessed=weight * 15_000_000, transcendentals=0),
    )(*operands)


def copy_to(source, target, sem):
    copy = pltpu.make_async_copy(source, target, sem)
    copy.start()
    return copy


def copy_rows(refs, held, sems):
    zl, y, x, zh, c, p, h = me()
    z = zh * 2 + zl
    copies = []
    for step, ref in enumerate(refs):
        at = lax.rem(z + (1 - c) * (8 - step) + c * step, 8)
        spot = flip(lax.rem(at, 2), lax.div(x, 2)) * 4 + lax.div(at, 2)
        copies.append(copy_to(ref, held.at[spot], sems.at[step]))
    return copies


def back_to_inputs(rows, weights, starts, halves, got=None):
    piece, n = rows[0].shape
    lanes = weights[0].shape[0]
    block = jax.ShapeDtypeStruct((4 * piece, 4 * lanes), jnp.bfloat16)
    both = jax.ShapeDtypeStruct((2,) + block.shape, jnp.bfloat16)

    def body(ins, outs, scratch):
        held_rows, held_weights, sems = scratch[:3]
        zl, y, x, zh, c, p, h = me()
        copies = []
        for i in range(8):
            at, core = lax.rem(y + (0, 3, 1, 2)[i % 4], 4), (c, 1 - c)[i // 4]
            spot = flip(lax.div(at, 2), h) * 4 + flip(lax.rem(at, 2), lax.rem(y, 2)) * 2 + core
            source = ins[8 + i].at[:, starts[i] : starts[i] + n]
            copies.append(copy_to(source, held_weights.at[spot], sems.at[8 + i]))
        copies += copy_rows(ins[:8], held_rows, sems)
        if got is not None:
            copies.append(copy_to(ins[16], scratch[3], sems.at[16]))

        def finish():
            for copy in copies:
                copy.wait()
            for i, (t, f) in enumerate(halves):
                a = held_rows[4 * t : 4 * t + 4].reshape(4 * piece, n)
                b = held_weights[4 * f : 4 * f + 4].reshape(4 * lanes, n)
                value = dot(a, b, ((1,), (1,)))
                if got is None:
                    outs[0][i] = value.astype(jnp.bfloat16)
                else:
                    outs[i][...] = (value + scratch[3][i].astype(jnp.float32)).astype(jnp.bfloat16)

        return finish

    scratch = [
        pltpu.VMEM((8, piece, n), jnp.bfloat16),
        pltpu.VMEM((8, lanes, n), jnp.bfloat16),
        pltpu.SemaphoreType.DMA((17,)),
    ]
    operands = list(rows) + list(weights)
    if got is None:
        return operands, [both], scratch, body
    return operands + [got], [block, block], scratch + [pltpu.VMEM(both.shape, jnp.bfloat16)], body


def back_to_weights(rows, pieces, places, width, got=None):
    piece, n = rows[0].shape
    lanes = pieces[0].shape[-1] // 2

    def body(ins, outs, scratch):
        held_rows, held_pieces, turned, sems = scratch[:4]
        zl, y, x, zh, c, p, h = me()
        core = 1 - c if got is None else c
        copies = []
        for i, (token, feature) in enumerate(places):
            half = flip(h, feature)
            for r in range(2):
                rel_p = flip(flip(half, flip(lax.rem(y, 2), r)), p)
                order = rel_p * 2 + flip(half, lax.div(y, 2))
                source = ins[8 + i].at[r, :, pl.ds(pl.multiple_of(core * lanes, lanes), lanes)]
                target = held_pieces.at[order, pl.ds(token * 4 * piece, 4 * piece), :]
                copies.append(copy_to(source, target, sems.at[8 + 2 * i + r]))
        row_copies = copy_rows(ins[:8], held_rows, sems)
        if got is not None:
            row_copies.append(copy_to(ins[12], scratch[4], sems.at[16]))

        def finish():
            for copy in copies:
                copy.wait()
            for i in range(4):
                turned[i * lanes : (i + 1) * lanes, :] = held_pieces[i].T
            for copy in row_copies:
                copy.wait()
            for i in range(n // width):
                cols = held_rows[:, :, i * width : (i + 1) * width].reshape(8 * piece, width)
                value = dot(turned[...], cols, ((1,), (0,)))
                if got is None:
                    outs[0][:, i * width : (i + 1) * width] = value.astype(jnp.bfloat16)
                    continue
                value = value + scratch[4][:, i * width : (i + 1) * width].astype(jnp.float32)
                value = value.astype(jnp.bfloat16)
                second = i * width >= n // 2
                at = i * width - (n // 2 if second else 0)
                for j in range(4):
                    away, spot = (j % 2, j // 2) if second else (j // 2, j % 2)
                    out = outs[2 * second + away]
                    out[spot * lanes : (spot + 1) * lanes, at : at + width] = value[j * lanes : (j + 1) * lanes]

        return finish

    scratch = [
        pltpu.VMEM((8, piece, n), jnp.bfloat16),
        pltpu.VMEM((4, 8 * piece, lanes), jnp.bfloat16),
        pltpu.VMEM((4 * lanes, 8 * piece), jnp.bfloat16),
        pltpu.SemaphoreType.DMA((17,)),
    ]
    whole = jax.ShapeDtypeStruct((4 * lanes, n), jnp.bfloat16)
    quarter = jax.ShapeDtypeStruct((2 * lanes, n // 2), jnp.bfloat16)
    operands = list(rows) + list(pieces)
    if got is None:
        return operands, [whole], scratch, body
    return operands + [got], [quarter] * 4, scratch + [pltpu.VMEM(whole.shape, jnp.bfloat16)], body


def body(layer_input, core_output, grad_qkv, grad_out, w_qkv, w_out):
    yl = lax.rem(lax.axis_index("y"), 2)
    piece = grad_qkv.shape[0]
    lanes = w_qkv.shape[0]
    sizes = [w_qkv.shape[1], w_out.shape[1]]

    held = [grad_qkv, grad_out]
    rows = [[grad_qkv], [grad_out]]

    def hop():
        for i in range(2):
            held[i] = permute(held[i], ring_z)
            rows[i].append(held[i])

    def due(*values):
        held[1] = tie(held[1], *values)[0]

    def later(*values):
        return tie(*values, *held)[:-2]

    own = jnp.concatenate([w_qkv, w_out], 1)
    hop()
    low = permute(own, shift_y(1))
    high = permute(own, shift_y(-1))
    xs = jnp.stack([layer_input, core_output]).reshape(2, 2, piece, 4, 2 * lanes)
    xs = xs.transpose(3, 1, 0, 2, 4)
    xs = swap_blocks(xs)
    across = [permute(low[:, : sizes[0]], shift_y(1)), permute(high[:, sizes[0] :], shift_y(-1))]
    hop()
    hop()
    spread = [permute(either(flip(yl, r), xs[:, 0], xs[:, 1]), spread_xy(r)) for r in range(2)]
    far = [permute(v, other_core) for v in (own, low, high)]
    hop()
    hop()
    far += [permute(v, other_core) for v in across]
    first = [jnp.stack([v[:, i].reshape(4 * piece, 2 * lanes) for v in spread]) for i in range(2)]
    second = [permute(first[0], pair_x(3)), permute(first[1], pair_x(1))]
    hop()
    third = [jnp.stack([first[i], second[i]]) for i in range(2)]
    third = [permute(third[0], pair_x(1)), permute(third[1], pair_x(3))]
    hop()
    weights = [[own, low, high, across[i], *far[:3], far[3 + i]] for i in range(2)]
    starts = [[0] * 8, [sizes[0], sizes[0], sizes[0], 0] * 2]

    pieces = [[first[a], second[a], third[a][0], third[a][1]] for a in range(2)]
    places = [[(0, 0), (1, 0), (0, 1), (1, 1)], [(0, 0), (0, 1), (1, 0), (1, 1)]]
    widths = [384, 256]

    one, two = run(
        1,
        back_to_inputs(rows[0], weights[0], starts[0], [(0, 1), (1, 1)]),
        back_to_inputs(rows[1], weights[1], starts[1], [(1, 0), (1, 1)]),
    )
    one_got, two_got = permute(one, pair_x(1)), permute(two, pair_x(3))
    rows[0][0] = tie(rows[0][0], one)[0]
    w_one, w_two = run(6, *[back_to_weights(rows[a], pieces[a], places[a], widths[a]) for a in range(2)])
    w_got = [permute(w_one, other_core), permute(w_two, other_core)]
    one, one_sent, two, two_sent = run(
        6,
        back_to_inputs(rows[0], weights[0], starts[0], [(0, 0), (1, 0)], one_got),
        back_to_inputs(rows[1], weights[1], starts[1], [(0, 0), (0, 1)], two_got),
    )
    one_got, two_got = permute(one_sent, pair_x(3)), permute(two_sent, pair_x(1))
    outs = run(6, *[back_to_weights(rows[a], pieces[a], places[a], widths[a], w_got[a]) for a in range(2)])
    kept = [[outs[4 * a], outs[4 * a + 2]] for a in range(2)]
    y_got = [[permute(outs[4 * a + 1], pair_y(1)), permute(outs[4 * a + 3], pair_y(3))] for a in range(2)]
    one_got, two_got, _ = tie(one_got, two_got, outs[0])

    total = [add(one, one_got), add(two, two_got)]
    total = jnp.stack([v.reshape(4, piece, 4 * lanes) for v in total], 1)
    back = [permute(total[..., r * 2 * lanes : (r + 1) * 2 * lanes], collect_xy(r)) for r in range(2)]
    done = []
    for a in range(2):
        sent = [add(k[lanes:], g[lanes:]) for k, g in zip(kept[a], y_got[a])]
        kept[a] = [add(k[:lanes], g[:lanes]) for k, g in zip(kept[a], y_got[a])]
        y_got[a] = [permute(sent[0], pair_y(3)), permute(sent[1], pair_y(1))]
    back = jnp.stack([either(yl, *back), either(yl, back[1], back[0])], 1)
    back = swap_blocks(back)
    for a in range(2):
        done.append(jnp.concatenate([add(k, g) for k, g in zip(kept[a], y_got[a])], -1))
    out = [jnp.concatenate([back[k, :, i] for k in range(4)], -1).reshape(2 * piece, 8 * lanes) for i in range(2)]
    return out[0], out[1], done[0], done[1]


def solution(mesh):
    fine = Mesh(mesh.devices.reshape(SIZES), AXES)
    inputs = P(("zh", "c", "x"), ("zl", "y"))
    grads = P(("zh", "c", "zl", "y"), "x")
    weights = P(("zl", "y", "zh", "c"), "x")
    return jax.shard_map(
        body,
        mesh=fine,
        in_specs=(inputs, inputs, grads, grads, weights, weights),
        out_specs=(inputs, inputs, weights, weights),
        check_vma=False,
    )
```

```python
import jax
import jax.numpy as jnp
from jax import lax
from jax.experimental import pallas as pl
from jax.experimental.pallas import tpu as pltpu
from jax.sharding import Mesh, PartitionSpec as P

AXES = ("zl", "y", "x", "zh", "c")
SIZES = (2, 4, 4, 4, 2)


def place(i):
    return (i // 128) % 2, (i // 32) % 4, (i // 8) % 4, (i // 2) % 4, i % 2


def number(zl, y, x, zh, c):
    return (((zl * 4 + y) * 4 + x) * 4 + zh) * 2 + c


def permute(value, target):
    pairs = [(i, number(*target(*place(i)))) for i in range(256)]
    return lax.ppermute(value, AXES, pairs)


def pair_x(r):
    return lambda zl, y, x, zh, c: (zl, y, x ^ r, zh, c)


def pair_y(r):
    return lambda zl, y, x, zh, c: (zl, y ^ r, x, zh, c)


def other_core(zl, y, x, zh, c):
    return zl, y, x, zh, 1 - c


def shift_y(step):
    return lambda zl, y, x, zh, c: (zl, (y + step) % 4, x, zh, c)


def shift_z(step):
    def target(zl, y, x, zh, c):
        z = (zh * 2 + zl + step) % 8
        return z % 2, y, x, z // 2, c

    return target


def spread_xy(r):
    def target(zl, y, x, zh, c):
        xh, xl, yh, yl = x // 2, x % 2, y // 2, y % 2
        return zl, xl * 2 + (yl ^ r), xh * 2 + (yh ^ xh), zh, c

    return target


def collect_xy(r):
    def target(zl, y, x, zh, c):
        xh, xl, yh, yl = x // 2, x % 2, y // 2, y % 2
        return zl, (xl ^ xh) * 2 + (yl ^ r), xh * 2 + yh, zh, c

    return target


def swap_blocks(value):
    return lax.all_to_all(value, "zh", 0, 0, tiled=True)


def either(bit, first, second):
    return jnp.where(bit == 0, first, second)


def flip(a, b):
    return lax.rem(a + b, 2)


def add(a, b):
    return (a.astype(jnp.float32) + b.astype(jnp.float32)).astype(jnp.bfloat16)


def tie(*values):
    return lax.optimization_barrier(values)


def dot(a, b, on):
    return lax.dot_general(a, b, (on, ((), ())), preferred_element_type=jnp.float32)


def me():
    zl, y, x, zh, c = (lax.axis_index(a) for a in AXES)
    p = flip(lax.div(y, 2), lax.rem(y, 2))
    h = flip(lax.div(x, 2), lax.rem(x, 2))
    return zl, y, x, zh, c, p, h


def run(weight, *jobs):
    operands = [v for job in jobs for v in job[0]]
    outs = [v for job in jobs for v in job[1]]

    def kernel(*refs):
        at = [0, len(operands), len(operands) + len(outs)]
        stages = []
        for ins, out, scratch, body in jobs:
            parts = []
            for i, v in enumerate((ins, out, scratch)):
                parts.append(refs[at[i] : at[i] + len(v)])
                at[i] += len(v)
            stages.append(body(*parts))
        for finish in stages:
            finish()

    return pl.pallas_call(
        kernel,
        out_shape=outs,
        in_specs=[pl.BlockSpec(memory_space=pl.ANY)] * len(operands),
        out_specs=[pl.BlockSpec(memory_space=pltpu.VMEM)] * len(outs),
        scratch_shapes=[v for job in jobs for v in job[2]],
        compiler_params=pltpu.CompilerParams(vmem_limit_bytes=48 * 1024 * 1024),
        cost_estimate=pl.CostEstimate(flops=weight * 3_400_000_000, bytes_accessed=weight * 15_000_000, transcendentals=0),
    )(*operands)


def copy_to(source, target, sem):
    copy = pltpu.make_async_copy(source, target, sem)
    copy.start()
    return copy


def copy_rows(refs, starts, held, sems):
    zl, y, x, zh, c, p, h = me()
    n = held.shape[2]
    copies = []
    for i, (ref, step) in enumerate(zip(refs, (0, 7, 6, 5, 1, 2, 3, 4))):
        at = lax.rem(zh * 2 + zl + step, 8)
        spot = flip(lax.rem(at, 2), lax.div(x, 2)) * 4 + lax.div(at, 2)
        copies.append(copy_to(ref.at[:, starts[i] : starts[i] + n], held.at[spot], sems.at[i]))
    return copies


def back_to_inputs(rows, row_starts, weights, starts, halves, got=None):
    piece, n = rows[7].shape
    lanes = weights[0].shape[0]
    block = jax.ShapeDtypeStruct((4 * piece, 4 * lanes), jnp.bfloat16)
    both = jax.ShapeDtypeStruct((2,) + block.shape, jnp.bfloat16)

    def body(ins, outs, scratch):
        held_rows, held_weights, sems = scratch[:3]
        zl, y, x, zh, c, p, h = me()
        copies = []
        for i in range(8):
            at, core = lax.rem(y + (0, 3, 1, 2)[i % 4], 4), (c, 1 - c)[i // 4]
            spot = flip(lax.div(at, 2), h) * 4 + flip(lax.rem(at, 2), lax.rem(y, 2)) * 2 + core
            source = ins[8 + i].at[:, starts[i] : starts[i] + n]
            copies.append(copy_to(source, held_weights.at[spot], sems.at[8 + i]))
        copies += copy_rows(ins[:8], row_starts, held_rows, sems)
        if got is not None:
            copies.append(copy_to(ins[16], scratch[3], sems.at[16]))

        def finish():
            for copy in copies:
                copy.wait()
            for i, (t, f) in enumerate(halves):
                a = held_rows[4 * t : 4 * t + 4].reshape(4 * piece, n)
                b = held_weights[4 * f : 4 * f + 4].reshape(4 * lanes, n)
                value = dot(a, b, ((1,), (1,)))
                if got is None:
                    outs[0][i] = value.astype(jnp.bfloat16)
                else:
                    outs[i][...] = (value + scratch[3][i].astype(jnp.float32)).astype(jnp.bfloat16)

        return finish

    scratch = [
        pltpu.VMEM((8, piece, n), jnp.bfloat16),
        pltpu.VMEM((8, lanes, n), jnp.bfloat16),
        pltpu.SemaphoreType.DMA((17,)),
    ]
    operands = list(rows) + list(weights)
    if got is None:
        return operands, [both], scratch, body
    return operands + [got], [block, block], scratch + [pltpu.VMEM(both.shape, jnp.bfloat16)], body


def back_to_weights(rows, row_starts, pieces, places, width, got=None):
    piece, n = rows[7].shape
    lanes = pieces[0].shape[-1] // 2

    def body(ins, outs, scratch):
        held_rows, held_pieces, turned, sems = scratch[:4]
        zl, y, x, zh, c, p, h = me()
        core = 1 - c if got is None else c
        copies = []
        for i, (token, feature) in enumerate(places):
            half = flip(h, feature)
            for r in range(2):
                rel_p = flip(flip(half, flip(lax.rem(y, 2), r)), p)
                order = rel_p * 2 + flip(half, lax.div(y, 2))
                source = ins[8 + i].at[r, :, pl.ds(pl.multiple_of(core * lanes, lanes), lanes)]
                target = held_pieces.at[order, pl.ds(token * 4 * piece, 4 * piece), :]
                copies.append(copy_to(source, target, sems.at[8 + 2 * i + r]))
        row_copies = copy_rows(ins[:8], row_starts, held_rows, sems)
        if got is not None:
            row_copies.append(copy_to(ins[12], scratch[4], sems.at[16]))

        def finish():
            for copy in copies:
                copy.wait()
            for i in range(4):
                turned[i * lanes : (i + 1) * lanes, :] = held_pieces[i].T
            for copy in row_copies:
                copy.wait()
            for i in range(n // width):
                cols = held_rows[:, :, i * width : (i + 1) * width].reshape(8 * piece, width)
                value = dot(turned[...], cols, ((1,), (0,)))
                if got is None:
                    outs[0][:, i * width : (i + 1) * width] = value.astype(jnp.bfloat16)
                    continue
                value = value + scratch[4][:, i * width : (i + 1) * width].astype(jnp.float32)
                value = value.astype(jnp.bfloat16)
                second = i * width >= n // 2
                at = i * width - (n // 2 if second else 0)
                for j in range(4):
                    away, spot = (j % 2, j // 2) if second else (j // 2, j % 2)
                    out = outs[2 * second + away]
                    out[spot * lanes : (spot + 1) * lanes, at : at + width] = value[j * lanes : (j + 1) * lanes]

        return finish

    scratch = [
        pltpu.VMEM((8, piece, n), jnp.bfloat16),
        pltpu.VMEM((4, 8 * piece, lanes), jnp.bfloat16),
        pltpu.VMEM((4 * lanes, 8 * piece), jnp.bfloat16),
        pltpu.SemaphoreType.DMA((17,)),
    ]
    whole = jax.ShapeDtypeStruct((4 * lanes, n), jnp.bfloat16)
    quarter = jax.ShapeDtypeStruct((2 * lanes, n // 2), jnp.bfloat16)
    operands = list(rows) + list(pieces)
    if got is None:
        return operands, [whole], scratch, body
    return operands + [got], [quarter] * 4, scratch + [pltpu.VMEM(whole.shape, jnp.bfloat16)], body


def body(layer_input, core_output, grad_qkv, grad_out, w_qkv, w_out):
    yl = lax.rem(lax.axis_index("y"), 2)
    piece = grad_qkv.shape[0]
    lanes = w_qkv.shape[0]
    sizes = [w_qkv.shape[1], w_out.shape[1]]

    grads = jnp.concatenate([grad_qkv, grad_out], 1)
    split = grad_qkv.shape[1]
    ways = [[grads], [grads]]
    for _ in range(3):
        for way, step in zip(ways, (1, -1)):
            way.append(permute(way[-1], shift_z(step)))
    last = [permute(ways[0][3][:, :split], shift_z(1)), permute(ways[1][3][:, split:], shift_z(-1))]
    rows = [[grads, *ways[0][1:], *ways[1][1:], last[a]] for a in range(2)]
    row_starts = [[0] * 8, [split] * 7 + [0]]

    own = jnp.concatenate([w_qkv, w_out], 1)
    xs = jnp.stack([layer_input, core_output]).reshape(2, 2, piece, 8 * lanes)
    spread = [permute(either(flip(yl, r), xs[:, 0], xs[:, 1]), spread_xy(r)) for r in range(2)]
    xs = jnp.stack(spread).reshape(2, 2, piece, 4, 2 * lanes).transpose(3, 1, 0, 2, 4)
    xs = tie(xs, ways[0][1], ways[1][1])[0]
    xs = swap_blocks(xs)
    first = [xs[:, a].transpose(1, 0, 2, 3).reshape(2, 4 * piece, 2 * lanes) for a in range(2)]
    low = permute(own, shift_y(1))
    high = permute(own, shift_y(-1))
    across = [permute(low[:, : sizes[0]], shift_y(1)), permute(high[:, sizes[0] :], shift_y(-1))]
    far = [permute(v, other_core) for v in (own, low, high, *across)]
    second = [permute(first[0], pair_x(3)), permute(first[1], pair_x(1))]
    third = [jnp.stack([first[i], second[i]]) for i in range(2)]
    third = [permute(third[0], pair_x(1)), permute(third[1], pair_x(3))]
    weights = [[own, low, high, across[i], *far[:3], far[3 + i]] for i in range(2)]
    starts = [[0] * 8, [sizes[0], sizes[0], sizes[0], 0] * 2]

    pieces = [[first[a], second[a], third[a][0], third[a][1]] for a in range(2)]
    places = [[(0, 0), (1, 0), (0, 1), (1, 1)], [(0, 0), (0, 1), (1, 0), (1, 1)]]
    widths = [384, 256]

    one, two = run(
        1,
        back_to_inputs(rows[0], row_starts[0], weights[0], starts[0], [(0, 1), (1, 1)]),
        back_to_inputs(rows[1], row_starts[1], weights[1], starts[1], [(1, 0), (1, 1)]),
    )
    one_got, two_got = permute(one, pair_x(1)), permute(two, pair_x(3))
    rows[0][0] = tie(rows[0][0], one)[0]
    w_one, w_two = run(6, *[back_to_weights(rows[a], row_starts[a], pieces[a], places[a], widths[a]) for a in range(2)])
    w_got = [permute(w_one, other_core), permute(w_two, other_core)]
    one, one_sent, two, two_sent = run(
        6,
        back_to_inputs(rows[0], row_starts[0], weights[0], starts[0], [(0, 0), (1, 0)], one_got),
        back_to_inputs(rows[1], row_starts[1], weights[1], starts[1], [(0, 0), (0, 1)], two_got),
    )
    one_got, two_got = permute(one_sent, pair_x(3)), permute(two_sent, pair_x(1))
    outs = run(6, *[back_to_weights(rows[a], row_starts[a], pieces[a], places[a], widths[a], w_got[a]) for a in range(2)])
    kept = [[outs[4 * a], outs[4 * a + 2]] for a in range(2)]
    y_got = [[permute(outs[4 * a + 1], pair_y(1)), permute(outs[4 * a + 3], pair_y(3))] for a in range(2)]
    one_got, two_got, _ = tie(one_got, two_got, outs[0])

    total = [add(one, one_got), add(two, two_got)]
    total = jnp.stack([v.reshape(4, piece, 4 * lanes) for v in total], 1)
    back = [permute(total[..., r * 2 * lanes : (r + 1) * 2 * lanes], collect_xy(r)) for r in range(2)]
    done = []
    for a in range(2):
        sent = [add(k[lanes:], g[lanes:]) for k, g in zip(kept[a], y_got[a])]
        kept[a] = [add(k[:lanes], g[:lanes]) for k, g in zip(kept[a], y_got[a])]
        y_got[a] = [permute(sent[0], pair_y(3)), permute(sent[1], pair_y(1))]
    back = jnp.stack([either(yl, *back), either(yl, back[1], back[0])], 1)
    back = swap_blocks(back)
    for a in range(2):
        done.append(jnp.concatenate([add(k, g) for k, g in zip(kept[a], y_got[a])], -1))
    out = [jnp.concatenate([back[k, :, i] for k in range(4)], -1).reshape(2 * piece, 8 * lanes) for i in range(2)]
    return out[0], out[1], done[0], done[1]


def solution(mesh):
    fine = Mesh(mesh.devices.reshape(SIZES), AXES)
    inputs = P(("zh", "c", "x"), ("zl", "y"))
    grads = P(("zh", "c", "zl", "y"), "x")
    weights = P(("zl", "y", "zh", "c"), "x")
    return jax.shard_map(
        body,
        mesh=fine,
        in_specs=(inputs, inputs, grads, grads, weights, weights),
        out_specs=(inputs, inputs, weights, weights),
        check_vma=False,
    )
```
